32 devices in a mesh: dp: 8 (over z, core), mp: 4 (over y, x).
Axes of the slice: x: 2, y: 2, z: 4, core: 2. Of those that a mesh axis runs over, the one named last changes fastest.
Arguments:
- inputs: bfloat16 [2, 8, 2308, 1024], P(None, 'dp', 'mp'), may hold values from -6 to 6
- cotangent: bfloat16 [2, 8, 2308, 1024], P(None, 'dp', 'mp'), may hold values from -6 to 6
- counts: int32 [2, 8], P(None, 'dp'), may hold values from 1 to 4, as said below
- qkv_weight: bfloat16 [1024, 3, 1024], P('dp', None, 'mp'), may hold values from -0.1875 to 0.1875
- qv_bias: bfloat16 [2, 1024], P(None, 'mp'), may hold values from -0.75 to 0.75
- out_weight: bfloat16 [1024, 1024], P('mp', 'dp'), may hold values from -1.5 to 1.5
- up_weight: bfloat16 [1024, 4096], P('dp', 'mp'), may hold values from -0.1875 to 0.1875
- up_bias: bfloat16 [4096], P('mp'), may hold values from -4 to 4
- down_weight: bfloat16 [4096, 1024], P('mp', 'dp'), may hold values from -0.09375 to 0.09375
- norm_gain: bfloat16 [2, 1024], P(None, 'dp'), may hold values from 0.099609375 to 1.8984375
- norm_shift: bfloat16 [2, 1024], P(None, 'dp'), may hold values from -4 to 4
- out_bias: bfloat16 [2, 1024], P(None, 'dp'), may hold values from -4 to 4
Outputs:
- outputs: bfloat16 [2, 8, 2308, 1024], P(None, 'dp', 'mp')
- input_grad: float32 [2, 8, 2308, 1024], P(None, 'dp', 'mp')
- qkv_grad: float32 [1024, 3, 1024], P('dp', None, 'mp')
- qv_bias_grad: float32 [2, 1024], P(None, 'mp')
- out_weight_grad: float32 [1024, 1024], P('mp', 'dp')
- up_weight_grad: float32 [1024, 4096], P('dp', 'mp')
- up_bias_grad: float32 [4096], P('mp')
- down_weight_grad: float32 [4096, 1024], P('mp', 'dp')
- norm_gain_grad: float32 [2, 1024], P(None, 'dp')
- norm_shift_grad: float32 [2, 1024], P(None, 'dp')
- out_bias_grad: float32 [2, 1024], P(None, 'dp')
The draws below stay inside these ranges and needn't reach their ends.
Inputs may be any that keep to these rules, and one draw needn't show every extreme that they name: Slots 0 to counts - 1 of a group hold its images; in each micro-batch some data group holds all 4.
All inputs are finite; a program needn't handle non-finite values.
Results may differ from the reference program's by a relative error of at most 0.02.
Values may be sent and summed in bfloat16 or wider, within the bound.
A program may use at most 448 MiB of HBM per device.

```python
import jax
import jax.numpy as jnp
from jax import lax

D = 1024
HEADS = 16
HEAD_DIM = 64
FF = 4096
SEQ = 577
MB = 2
CAP = 4
GROUPS = 8
N_MP = 4


def draw_counts(key, part):
    first_key = jax.random.fold_in(key, 11)
    second_key = jax.random.fold_in(key, 23)
    drawn = jax.random.randint(first_key, (MB, GROUPS), 1, CAP + 1)
    chosen = jax.random.randint(second_key, (MB, 1), 0, GROUPS)
    column = jnp.arange(GROUPS, dtype=jnp.int32)[None, :]
    return jnp.where(column == chosen, CAP, drawn).astype(jnp.int32)


def levels(own_key, shape, pieces, least, top_value):
    def one(position, shards_of):
        heights = jax.random.uniform(jax.random.fold_in(jax.random.fold_in(own_key, 6), position), (shards_of,), jnp.float32, least / len(pieces), top_value / len(pieces))
        return jnp.repeat(jnp.exp(heights), shape[position] // shards_of).reshape((-1,) + (1,) * (len(shape) - position - 1))

    level = one(*pieces[0])
    for cut in pieces[1:]:
        level = level * one(*cut)
    return level


def gaussian(key, dims, width, bound, shards=(), kind=jnp.bfloat16):
    factor_of = levels(key, dims, shards, -0.22, 0.18) if shards else 1.0
    entries = jax.random.normal(key, dims, jnp.float32) * width * factor_of
    return jnp.minimum(jnp.maximum(entries, -bound), bound).astype(kind)


def setup_inputs(seed: int = 0) -> dict:
    key_of = jax.random.split(jax.random.key(seed), 13)
    return {
        "inputs": gaussian(key_of[0], (MB, GROUPS, CAP * SEQ, D), 1.0, 6.0, ((1, 8), (2, 4))),
        "cotangent": gaussian(key_of[1], (MB, GROUPS, CAP * SEQ, D), 1.0, 6.0, ((1, 8), (2, 4))),
        "counts": draw_counts(jax.random.fold_in(key_of[12], 71), 0),
        "qkv_weight": gaussian(key_of[3], (D, 3, D), D ** -0.5, 0.1875, ((0, 8), (2, 4))),
        "qv_bias": gaussian(key_of[4], (2, D), 0.05, 0.75, ((1, 4),)),
        "out_weight": gaussian(key_of[5], (D, D), 16 ** -0.5, 1.5, ((0, 4), (1, 8))),
        "up_weight": gaussian(key_of[6], (D, FF), D ** -0.5, 0.1875, ((0, 8), (1, 4))),
        "up_bias": gaussian(key_of[7], (FF,), 0.3, 4.0, ((0, 4),)),
        "down_weight": gaussian(key_of[8], (FF, D), FF ** -0.5, 0.09375, ((0, 4), (1, 8))),
        "norm_gain": jnp.clip(1.0 + 0.18 * jax.random.normal(key_of[9], (2, D), jnp.float32), 0.099609375, 1.8984375).astype(jnp.bfloat16),
        "norm_shift": gaussian(key_of[10], (2, D), 0.3, 4.0, ((1, 8),)),
        "out_bias": gaussian(key_of[11], (2, D), 0.3, 4.0, ((1, 8),)),
    }


norm_eps = 1e-06
highest = lax.Precision.HIGHEST

@jax.custom_vjp
def low(v):
    return lax.optimization_barrier(v.astype(jnp.bfloat16)).astype(jnp.float32)

@jax.custom_vjp
def low_back(v):
    return v

def low_keep(v):
    return (low(v), None)

def low_pass(kept, grad):
    return (grad,)

def back_keep(v):
    return (v, None)

def back_low(kept, grad):
    return (low(grad),)
low.defvjp(low_keep, low_pass)
low_back.defvjp(back_keep, back_low)

def normalize(values, gain, shift):
    center = lax.optimization_barrier(jnp.mean(values, axis=-1, keepdims=True))
    centered = values - center
    spread = lax.optimization_barrier(jnp.mean(centered * centered, axis=-1, keepdims=True))
    return centered * lax.rsqrt(spread + norm_eps) * gain + shift

def grouped_sum(left, right):
    parts = jnp.einsum('sgf,gfe->sge', left.reshape(left.shape[0], N_MP, -1), right.reshape(N_MP, -1, right.shape[1]), precision=highest)
    return lax.optimization_barrier(jnp.sum(low(parts), axis=1))

def layer(image, params):
    qkv_weight, qv_bias, out_weight, up_weight, up_bias, down_weight, norm_gain, norm_shift, out_bias = params
    first = low(normalize(image, norm_gain[0], norm_shift[0]))
    query = low(low_back(jnp.dot(first, qkv_weight[:, 0], precision=highest) + qv_bias[0]))
    key_rows = low(low_back(jnp.dot(first, qkv_weight[:, 1], precision=highest)))
    value = low(low_back(jnp.dot(first, qkv_weight[:, 2], precision=highest) + qv_bias[1]))
    split = (image.shape[0], HEADS, HEAD_DIM)
    scores = low_back(jnp.einsum('qhd,khd->hqk', query.reshape(split), key_rows.reshape(split), precision=highest) * HEAD_DIM ** (-0.5))
    weights = low(jax.nn.softmax(scores, axis=-1))
    mixed = low(low_back(jnp.einsum('hqk,khd->qhd', weights, value.reshape(split), precision=highest).reshape(image.shape)))
    middle = image + low_back(grouped_sum(mixed, out_weight)) + out_bias[0]
    second = low(normalize(middle, norm_gain[1], norm_shift[1]))
    hidden = low_back(jnp.dot(second, up_weight, precision=highest) + up_bias)
    act = low(jax.nn.gelu(hidden, approximate=False))
    return middle + low_back(grouped_sum(act, down_weight)) + out_bias[1]

def reference(inputs, cotangent, counts, qkv_weight, qv_bias, out_weight, up_weight, up_bias, down_weight, norm_gain, norm_shift, out_bias):
    params = tuple((item.astype(jnp.float32) for item in (qkv_weight, qv_bias, out_weight, up_weight, up_bias, down_weight, norm_gain, norm_shift, out_bias)))
    total_images = MB * GROUPS * CAP
    images = inputs.astype(jnp.float32).reshape(total_images, SEQ, D)
    pulls = cotangent.astype(jnp.float32).reshape(total_images, SEQ, D)
    slots = jnp.arange(CAP, dtype=jnp.int32)
    alive = (slots[None, None, :] < counts.astype(jnp.int32)[:, :, None]).reshape(total_images)

    def advance(totals, item):
        image, pull_in, alive_flag = item
        result, backward = jax.vjp(layer, image, params)
        weight_live = jnp.where(alive_flag, 1.0, 0.0).astype(jnp.float32)
        image_grad, param_grads = backward(pull_in * weight_live)
        totals = jax.tree.map(lambda a, b: a + b, totals, param_grads)
        return (totals, ((result * weight_live).astype(jnp.bfloat16), image_grad))
    zeros = jax.tree.map(jnp.zeros_like, params)
    totals, (outputs, input_grad) = lax.scan(advance, zeros, (images, pulls, alive))
    shape = (MB, GROUPS, CAP * SEQ, D)
    return (outputs.reshape(shape), input_grad.reshape(shape), totals[0], totals[1], totals[2], totals[3], totals[4], totals[5], totals[6], totals[7], totals[8])
```

```python
import jax
import jax.numpy as jnp
from jax import lax
from jax.experimental import pallas as pl
from jax.experimental.pallas import tpu as pltpu
from jax.sharding import PartitionSpec as P

HEAD_DIM = 64
PAIR = 128


norm_eps = 1e-06
half_root = 0.7071067811865476
density_scale = 0.3989422804014327


def transposed_product(left, right):
    return lax.dot_general(
        left, right, (((0,), (0,)), ((), ())), preferred_element_type=jnp.float32
    )


def product_by_transpose(left, right):
    return lax.dot_general(
        left, right, (((1,), (1,)), ((), ())), preferred_element_type=jnp.float32
    )


def normalize(values, gain, shift):
    center = jnp.mean(values, axis=-1, keepdims=True)
    centered = values - center
    spread = jnp.mean(centered * centered, axis=-1, keepdims=True)
    inverse = lax.rsqrt(spread + norm_eps)
    normed = centered * inverse
    return (normed * gain + shift, normed, inverse)


def normalize_back(grad_result, normed, inverse, gain):
    scaled = grad_result * gain
    first_mean = jnp.mean(scaled, axis=-1, keepdims=True)
    second_mean = jnp.mean(scaled * normed, axis=-1, keepdims=True)
    return inverse * (scaled - first_mean - normed * second_mean)


def gelu_slope(values):
    return 0.5 * (1.0 + lax.erf(values * half_root)) + values * density_scale * jnp.exp(
        -0.5 * values * values
    )


def head_masks(rows):
    lane = lax.broadcasted_iota(jnp.int32, (rows, PAIR), 1)
    return (lane < HEAD_DIM, lane >= HEAD_DIM)


def attend_kernel(query_ref, key_ref, value_ref, mixed_ref, log_ref):
    query = query_ref[0] * jnp.bfloat16(HEAD_DIM**-0.5)
    key_block = key_ref[0]
    value = value_ref[0]
    masks = head_masks(query.shape[0])
    parts = []
    for head in range(2):
        own = jnp.where(masks[head], query, jnp.zeros_like(query))
        scores = product_by_transpose(key_block, own)
        top_score = jnp.max(scores, axis=0, keepdims=True)
        weights = jnp.exp(scores - top_score)
        totals = jnp.sum(weights, axis=0, keepdims=True)
        weights_low = (weights * (1.0 / totals)).astype(jnp.bfloat16)
        parts.append(transposed_product(weights_low, value))
        log_ref[0, 0, head : head + 1, :] = top_score + jnp.log(totals)
    mixed_ref[0] = jnp.where(masks[0], parts[0], parts[1]).astype(jnp.bfloat16)


def attend_back_kernel(
    query_ref, key_ref, value_ref, mixed_grad_ref, log_ref, query_out, key_out, value_out
):
    scale = HEAD_DIM**-0.5
    query = query_ref[0] * jnp.bfloat16(scale)
    key_block = key_ref[0]
    value = value_ref[0]
    mixed_grad = mixed_grad_ref[0]
    masks = head_masks(query.shape[0])
    query_parts, key_parts, value_parts = [], [], []
    for head in range(2):
        own = jnp.where(masks[head], query, jnp.zeros_like(query))
        own_grad = jnp.where(masks[head], mixed_grad, jnp.zeros_like(mixed_grad))
        scores = product_by_transpose(key_block, own)
        weights = jnp.exp(scores - log_ref[0, 0, head : head + 1, :])
        weight_grad = product_by_transpose(value, own_grad)
        value_parts.append(
            jnp.dot(weights.astype(jnp.bfloat16), own_grad, preferred_element_type=jnp.float32)
        )
        centre = jnp.sum(weights * weight_grad, axis=0, keepdims=True)
        score_grad = (weights * (weight_grad - centre)).astype(jnp.bfloat16)
        query_parts.append(transposed_product(score_grad, key_block))
        key_parts.append(jnp.dot(score_grad, own, preferred_element_type=jnp.float32))
    query_out[0] = (jnp.where(masks[0], *query_parts) * scale).astype(jnp.bfloat16)
    key_out[0] = (key_parts[0] + key_parts[1]).astype(jnp.bfloat16)
    value_out[0] = (value_parts[0] + value_parts[1]).astype(jnp.bfloat16)


def part_specs(rows, pairs):
    return [
        pl.BlockSpec((1, rows, PAIR), lambda b, h, c=c: (b, 0, c * pairs + h)) for c in range(3)
    ]


def attend(packed):
    images, rows, width3 = packed.shape
    pairs = width3 // (3 * PAIR)
    plain = pl.BlockSpec((1, rows, PAIR), lambda b, h: (b, 0, h))
    logs = pl.BlockSpec((1, 1, 2, rows), lambda b, h: (b, h, 0, 0))
    return pl.pallas_call(
        attend_kernel,
        grid=(images, pairs),
        in_specs=part_specs(rows, pairs),
        out_specs=[plain, logs],
        out_shape=[
            jax.ShapeDtypeStruct((images, rows, width3 // 3), jnp.bfloat16),
            jax.ShapeDtypeStruct((images, pairs, 2, rows), jnp.float32),
        ],
        compiler_params=pltpu.CompilerParams(vmem_limit_bytes=40 * 2**20),
        cost_estimate=pl.CostEstimate(
            flops=images * rows * rows * width3 * 8 // 3,
            bytes_accessed=images * rows * width3 * 3,
            transcendentals=images * pairs * 2 * rows * rows,
        ),
    )(packed, packed, packed)


def attend_back(packed, mixed_grad, logs_in):
    images, rows, width3 = packed.shape
    pairs = width3 // (3 * PAIR)
    plain = pl.BlockSpec((1, rows, PAIR), lambda b, h: (b, 0, h))
    logs = pl.BlockSpec((1, 1, 2, rows), lambda b, h: (b, h, 0, 0))
    return pl.pallas_call(
        attend_back_kernel,
        grid=(images, pairs),
        in_specs=part_specs(rows, pairs) + [plain, logs],
        out_specs=[plain] * 3,
        out_shape=[jax.ShapeDtypeStruct((images, rows, width3 // 3), jnp.bfloat16)] * 3,
        compiler_params=pltpu.CompilerParams(vmem_limit_bytes=48 * 2**20),
        cost_estimate=pl.CostEstimate(
            flops=images * rows * rows * width3 * 20 // 3,
            bytes_accessed=images * rows * width3 * 5,
            transcendentals=images * pairs * 2 * rows * rows,
        ),
    )(packed, packed, packed, mixed_grad, logs_in)


BOTH = ("dp", "mp")


def mm(left, right):
    return jnp.einsum("bsk,kn->bsn", left, right, preferred_element_type=jnp.float32)


def mmt(left, right):
    return jnp.einsum("bsn,kn->bsk", left, right, preferred_element_type=jnp.float32)


def gram(left, right):
    return jnp.einsum("bsk,bsn->kn", left, right, preferred_element_type=jnp.float32)


def column_sum(values):
    return jnp.sum(values, axis=(0, 1), dtype=jnp.float32)


def shards(
    inputs,
    cotangent,
    counts,
    qkv_weight,
    qv_bias,
    out_weight,
    up_weight,
    up_bias,
    down_weight,
    norm_gain,
    norm_shift,
    out_bias,
):
    dps, mps = lax.axis_size("dp"), lax.axis_size("mp")
    rows_dp, local_width = qkv_weight.shape[0], qkv_weight.shape[2]
    width = rows_dp * dps
    units_mp = up_weight.shape[1]
    units = units_mp * mps
    columns_dp = out_weight.shape[1]

    small = jnp.concatenate(
        [norm_gain.reshape(-1), norm_shift.reshape(-1), out_bias.reshape(-1)]
        + [qv_bias.reshape(-1), up_bias]
    )
    small_all = lax.all_gather(small, BOTH, axis=0, tiled=False).reshape(dps, mps, -1)
    qkv_all = lax.all_gather(qkv_weight, BOTH, axis=0, tiled=False)
    out_all = lax.all_gather(out_weight, BOTH, axis=0, tiled=False)
    up_all = lax.all_gather(up_weight, BOTH, axis=0, tiled=False)
    down_all = lax.all_gather(down_weight, BOTH, axis=0, tiled=False)

    split = 6 * columns_dp
    by_dp = small_all[:, 0, :split].reshape(dps, 6, columns_dp)
    by_dp = by_dp.transpose(1, 0, 2).reshape(6, width).astype(jnp.float32)
    gain_wide, shift_wide, bias_wide = by_dp[0:2], by_dp[2:4], by_dp[4:6]
    by_mp = small_all[0, :, split:].astype(jnp.float32)
    head_bias = by_mp[:, : 2 * local_width].reshape(mps, 2, local_width)
    head_bias = head_bias.transpose(1, 0, 2).reshape(2, width)
    unit_shift = by_mp[:, 2 * local_width :].reshape(units)
    qkv_shift = jnp.concatenate([head_bias[0], jnp.zeros_like(head_bias[0]), head_bias[1]])

    qkv_matrix = (
        qkv_all.reshape(dps, mps, rows_dp, 3, local_width)
        .transpose(0, 2, 3, 1, 4)
        .reshape(width, 3 * width)
    )
    out_full = (
        out_all.reshape(dps, mps, local_width, columns_dp)
        .transpose(1, 2, 0, 3)
        .reshape(width, width)
    )
    up_full = (
        up_all.reshape(dps, mps, rows_dp, units_mp).transpose(0, 2, 1, 3).reshape(width, units)
    )
    down_full = (
        down_all.reshape(dps, mps, units_mp, columns_dp)
        .transpose(1, 2, 0, 3)
        .reshape(units, width)
    )

    live = (lax.axis_index("mp") < counts)[:, :, None]
    source = inputs[:, 0].astype(jnp.float32)
    first, normed_one, inverse_one = normalize(source, gain_wide[0], shift_wide[0])
    first_low = first.astype(jnp.bfloat16)
    grad_low = jnp.where(live, cotangent[:, 0], jnp.zeros_like(cotangent[:, 0]))
    grad_out = grad_low.astype(jnp.float32)

    packed = (mm(first_low, qkv_matrix) + qkv_shift).astype(jnp.bfloat16)
    mixed, logs = attend(packed)
    middle = source + mm(mixed, out_full) + bias_wide[0]
    second, normed_two, inverse_two = normalize(middle, gain_wide[1], shift_wide[1])
    second_low = second.astype(jnp.bfloat16)
    hidden = mm(second_low, up_full) + unit_shift
    act = jax.nn.gelu(hidden, approximate=False).astype(jnp.bfloat16)

    down_part = (
        gram(act, grad_low)
        .astype(jnp.bfloat16)
        .reshape(mps, units_mp, dps, columns_dp)
        .transpose(2, 0, 1, 3)
        .reshape(dps * mps, units_mp, columns_dp)
    )
    down_weight_grad = lax.psum_scatter(down_part, BOTH, scatter_dimension=0, tiled=False)

    result = middle + mm(act, down_full) + bias_wide[1]
    outputs = jnp.where(live, result, 0.0).astype(jnp.bfloat16)

    act_grad = mmt(grad_low, down_full)
    hidden_grad = (act_grad * gelu_slope(hidden)).astype(jnp.bfloat16)
    up_part = (
        gram(second_low, hidden_grad)
        .astype(jnp.bfloat16)
        .reshape(dps, rows_dp, mps, units_mp)
        .transpose(0, 2, 1, 3)
        .reshape(dps * mps, rows_dp, units_mp)
    )
    up_weight_grad = lax.psum_scatter(up_part, BOTH, scatter_dimension=0, tiled=False)

    second_grad = mmt(hidden_grad, up_full)
    middle_grad = grad_out + normalize_back(second_grad, normed_two, inverse_two, gain_wide[1])
    branch_low = middle_grad.astype(jnp.bfloat16)
    out_part = (
        gram(mixed, branch_low)
        .astype(jnp.bfloat16)
        .reshape(mps, local_width, dps, columns_dp)
        .transpose(2, 0, 1, 3)
        .reshape(dps * mps, local_width, columns_dp)
    )
    out_weight_grad = lax.psum_scatter(out_part, BOTH, scatter_dimension=0, tiled=False)

    mixed_grad = mmt(branch_low, out_full).astype(jnp.bfloat16)
    grads = attend_back(packed, mixed_grad, logs)
    packed_grad = jnp.concatenate(grads, axis=2)
    qkv_part = (
        gram(first_low, packed_grad)
        .astype(jnp.bfloat16)
        .reshape(dps, rows_dp, 3, mps, local_width)
        .transpose(0, 3, 1, 2, 4)
        .reshape(dps * mps, rows_dp, 3, local_width)
    )
    qkv_grad = lax.psum_scatter(qkv_part, BOTH, scatter_dimension=0, tiled=False)
    first_grad = mmt(packed_grad, qkv_matrix)
    input_grad = middle_grad + normalize_back(first_grad, normed_one, inverse_one, gain_wide[0])

    sums = jnp.concatenate(
        [
            column_sum(first_grad * normed_one),
            column_sum(second_grad * normed_two),
            column_sum(first_grad),
            column_sum(second_grad),
            column_sum(middle_grad),
            column_sum(grad_out),
            column_sum(grads[0]),
            column_sum(grads[2]),
            column_sum(hidden_grad),
        ]
    )
    sums = lax.psum(sums, BOTH)
    six = sums[: 6 * width].reshape(6, width)
    six = lax.dynamic_slice_in_dim(six, lax.axis_index("dp") * columns_dp, columns_dp, 1)
    two = sums[6 * width : 8 * width].reshape(2, width)
    mp_index = lax.axis_index("mp")
    qv_bias_grad = lax.dynamic_slice_in_dim(two, mp_index * local_width, local_width, 1)
    up_bias_grad = lax.dynamic_slice_in_dim(sums[8 * width :], mp_index * units_mp, units_mp, 0)
    wide = jnp.float32
    return (
        outputs[:, None],
        input_grad[:, None],
        qkv_grad.astype(wide),
        qv_bias_grad,
        out_weight_grad.astype(wide),
        up_weight_grad.astype(wide),
        up_bias_grad,
        down_weight_grad.astype(wide),
        six[0:2],
        six[2:4],
        six[4:6],
    )


def solution(mesh):
    in_specs = (
        P(None, "dp", "mp", None),
        P(None, "dp", "mp", None),
        P(None, "dp"),
        P("dp", None, "mp"),
        P(None, "mp"),
        P("mp", "dp"),
        P("dp", "mp"),
        P("mp"),
        P("mp", "dp"),
        P(None, "dp"),
        P(None, "dp"),
        P(None, "dp"),
    )
    out_specs = (
        P(None, "dp", "mp", None),
        P(None, "dp", "mp", None),
        P("dp", None, "mp"),
        P(None, "mp"),
        P("mp", "dp"),
        P("dp", "mp"),
        P("mp"),
        P("mp", "dp"),
        P(None, "dp"),
        P(None, "dp"),
        P(None, "dp"),
    )
    return jax.shard_map(shards, mesh=mesh, in_specs=in_specs, out_specs=out_specs, check_vma=False)
```
